512 devices in a mesh: tm: 16 (over z), space: 32 (over x, y, core).
Axes of the slice: x: 4, y: 4, z: 16, core: 2. Of those that a mesh axis runs over, the one named last changes fastest.
Arguments:
- starts: float32 [16, 512, 4096], P('tm', 'space'), may hold values from -15 to 15
- kappa: float32 [512, 4096], P('space'), may hold values from 0.5 to 4
- velocity_x: float32 [512, 4096], P('space'), may hold values from -0.8 to 0.8
- velocity_y: float32 [512, 4096], P('space'), may hold values from -0.8 to 0.8
Outputs:
- corrected: float32 [16, 512, 4096], P('tm', 'space')
The draws below stay inside these ranges and needn't reach their ends.
All inputs are finite; a program needn't handle non-finite values.
Results may differ from the reference program's by a relative error of at most 0.0003.
Values sent between devices are 32-bit elements; how exact they have to be, the bound alone decides.
No kernel may reach another device: no remote copies, remote signals or barrier semaphores. Data moves between devices by JAX's collectives and lax.ppermute only.
A program may use at most 64 MiB of HBM per device.

```python
import math
import jax
import jax.numpy as jnp
from jax import lax

NX = 4096
STEPS = 2
SWEEPS = 8
SLICES = 16
NY = 512


def draw_starts(key, part):
    key = jax.random.fold_in(key, 11)
    shared_key, own_key = jax.random.split(key, 2)
    row_position = jnp.arange(NY, dtype=jnp.float32) / max(NY - 1, 1)
    row_scale = jnp.exp(math.log(3.0) * row_position)[None, :, None]
    shared_part = jax.random.truncated_normal(shared_key, -3.0, 3.0, (1, NY, NX), jnp.float32)
    own_part = jax.random.truncated_normal(own_key, -3.0, 3.0, (SLICES, NY, NX), jnp.float32)
    drawn = row_scale * (shared_part + 0.6 * own_part)
    return drawn


def block_levels(rng, dims, cuts, least, top_value):
    gain = 1.0
    for axis_at, blocks in cuts:
        draws = jax.random.uniform(jax.random.fold_in(jax.random.fold_in(rng, 6), axis_at), (blocks,), jnp.float32, least / len(cuts), top_value / len(cuts))
        gain = gain * jnp.repeat(jnp.exp(draws), dims[axis_at] // blocks).reshape((-1,) + (1,) * (len(dims) - 1 - axis_at))
    return gain


def setup_inputs(seed: int = 0) -> dict:
    keys = jax.random.split(jax.random.key(seed), 5)
    starts = draw_starts(jax.random.fold_in(keys[4], 71), 0)
    kappa = jnp.clip(jnp.exp(math.log(4.0) - 2.0794415 * jax.random.uniform(keys[1], (NY, NX), jnp.float32) ** block_levels(keys[1], (NY, NX), ((0, 32),), -0.2, 0.2)), 0.5, 4.0)
    velocity_x = jnp.clip(jax.random.uniform(keys[2], (NY, NX), jnp.float32, -0.8, 0.8) * block_levels(keys[2], (NY, NX), ((0, 32),), -0.4, 0.0), -0.8, 0.8)
    velocity_y = jnp.clip(jax.random.uniform(keys[3], (NY, NX), jnp.float32, -0.8, 0.8) * block_levels(keys[3], (NY, NX), ((0, 32),), -0.4, 0.0), -0.8, 0.8)
    return {"starts": starts, "kappa": kappa, "velocity_x": velocity_x, "velocity_y": velocity_y}


step_tau = 0.4

def chebyshev_weights(sweep_count):
    return [1.0 / (1.0 - 0.8 * math.cos(math.pi * (2 * order + 1) / (2.0 * sweep_count))) for order in range(sweep_count)]

def face_weights(kappa_pad):
    center = kappa_pad[1:-1, 1:-1]
    north_face = 0.5 * (center + kappa_pad[:-2, 1:-1])
    south_face = 0.5 * (center + kappa_pad[2:, 1:-1])
    west_face = 0.5 * (center + kappa_pad[1:-1, :-2])
    east_face = 0.5 * (center + kappa_pad[1:-1, 2:])
    return (north_face, south_face, west_face, east_face)

def apply_operator(padded, faces, diagonal, velocity_x, velocity_y):
    north_face, south_face, west_face, east_face = faces
    center = padded[..., 1:-1, 1:-1]
    north = padded[..., :-2, 1:-1]
    south = padded[..., 2:, 1:-1]
    west = padded[..., 1:-1, :-2]
    east = padded[..., 1:-1, 2:]
    beside = north_face * north + south_face * south + west_face * west + east_face * east
    carried = 0.5 * velocity_x * (east - west) + 0.5 * velocity_y * (south - north)
    return diagonal * center - step_tau * beside + step_tau * carried

def coefficients(gram_matrix, cross_matrix):
    slices_here = gram_matrix.shape[0]
    drift = cross_matrix - gram_matrix
    factor = jnp.linalg.cholesky(gram_matrix)
    step_terms = jnp.concatenate([cross_matrix[:, :-1] - gram_matrix[:, 1:], jnp.zeros((slices_here, 1), gram_matrix.dtype)], axis=1)

    def advance(carried, column):
        alpha_now, sigma_sum = carried
        right_side = sigma_sum + jnp.dot(drift, alpha_now, precision=lax.Precision.HIGHEST)
        alpha_next = alpha_now + jax.scipy.linalg.cho_solve((factor, True), right_side)
        return ((alpha_next, sigma_sum + column), alpha_now)
    zero_vec = jnp.zeros((slices_here,), gram_matrix.dtype)
    _, alphas = lax.scan(advance, (zero_vec, zero_vec), step_terms.T)
    order_ids = jnp.arange(slices_here)
    below_mask = jnp.where(order_ids[:, None] < order_ids[None, :], 1.0, 0.0).astype(gram_matrix.dtype)
    return alphas.T + below_mask

def reference(starts, kappa, velocity_x, velocity_y):
    kappa_pad = jnp.pad(kappa, 1)
    faces = face_weights(kappa_pad)
    diagonal = 1.0 + step_tau * (faces[0] + faces[1] + faces[2] + faces[3])
    weights = jnp.asarray(chebyshev_weights(SWEEPS), jnp.float32)
    previous = starts
    current = starts
    for time_step in range(STEPS):
        right_side = (4.0 * current - previous) / 3.0
        field_now = current
        for sweep_index in range(SWEEPS):
            padded = jnp.pad(field_now, ((0, 0), (1, 1), (1, 1)))
            field_now = field_now + weights[sweep_index] * (right_side - apply_operator(padded, faces, diagonal, velocity_x, velocity_y)) / diagonal
        previous, current = (current, field_now)
    change = current - starts
    ends = starts + change
    gram_matrix = jnp.einsum('krc,irc->ki', starts, starts, precision=lax.Precision.HIGHEST)
    cross_matrix = jnp.einsum('krc,irc->ki', starts, ends, precision=lax.Precision.HIGHEST)
    mix_weights = coefficients(gram_matrix, cross_matrix)
    return starts[0][None] + jnp.einsum('ij,irc->jrc', mix_weights, change, precision=lax.Precision.HIGHEST)
```

```python
import functools
import math

import jax
import jax.numpy as jnp
from jax import lax
from jax.experimental import pallas as pl
from jax.experimental.pallas import tpu as pltpu
from jax.sharding import PartitionSpec as P

STEPS = 2
SWEEPS = 8
TAU = 0.4
LANES = 128
DEPTH = STEPS * SWEEPS
TILES = 3
VMEM = 48 * 2**20

F32 = jnp.float32
BF16 = jnp.bfloat16


def chebyshev_weights():
    return [
        1.0 / (1.0 - 0.8 * math.cos(math.pi * (2 * k + 1) / (2.0 * SWEEPS)))
        for k in range(SWEEPS)
    ]


def call(body, outs, scratch=(), smem=0, n_in=1):
    specs = [pl.BlockSpec(memory_space=pltpu.SMEM)] * smem
    specs += [pl.BlockSpec(memory_space=pltpu.VMEM)] * (n_in - smem)
    return pl.pallas_call(
        body,
        out_shape=outs,
        in_specs=specs,
        out_specs=[pl.BlockSpec(memory_space=pltpu.VMEM)] * len(outs),
        scratch_shapes=list(scratch),
        compiler_params=pltpu.CompilerParams(vmem_limit_bytes=VMEM),
    )


def pack(blocks, pos_ref, x_ref, kappa_ref, vx_ref, vy_ref, a_ref, c_ref):
    lane = lax.broadcasted_iota(jnp.int32, (DEPTH, LANES), 1)
    zero = jnp.zeros((DEPTH, LANES), F32)

    def rim(left, right):
        return jnp.where(lane < DEPTH, right, jnp.where(lane >= LANES - DEPTH, left, 0.0))

    def tile(i):
        return x_ref[:, i * LANES : (i + 1) * LANES] if 0 <= i < 2 * blocks else zero

    for t in range(blocks):
        a_ref[t, 0] = tile(2 * t)
        a_ref[t, 1] = tile(2 * t + 1)
        a_ref[t, 2] = rim(tile(2 * t - 1), tile(2 * t + 2))
    t = pos_ref[0]
    for q, ref in enumerate((kappa_ref, vx_ref, vy_ref)):
        def at(i):
            return ref[:, pl.ds(pl.multiple_of(i * LANES, LANES), LANES)]

        left = jnp.where(t > 0, at(jnp.maximum(2 * t - 1, 0)), 0.0)
        right = jnp.where(t < blocks - 1, at(jnp.minimum(2 * t + 2, 2 * blocks - 1)), 0.0)
        c_ref[q, 0] = at(2 * t)
        c_ref[q, 1] = at(2 * t + 1)
        c_ref[q, 2] = rim(left, right)


def lane_shift(tiles, lane):
    back = [pltpu.roll(v, 1, 1) for v in tiles]
    fore = [pltpu.roll(v, LANES - 1, 1) for v in tiles]
    west = [jnp.where(lane == 0, back[(c + 2) % 3], back[c]) for c in range(3)]
    east = [jnp.where(lane == LANES - 1, fore[(c + 1) % 3], fore[c]) for c in range(3)]
    return west, east


def stencil(blocks, slabs, pos_ref, up_ref, own_ref, down_ref, out_ref):
    rows = 3 * DEPTH
    t, s = pos_ref[0], pos_ref[1]
    lane = lax.broadcasted_iota(jnp.int32, (rows, LANES), 1)
    row = lax.broadcasted_iota(jnp.int32, (rows, LANES), 0) + (s - 1) * DEPTH
    inside = (row >= 0) & (row < slabs * DEPTH)

    def whole(q, c):
        return jnp.concatenate([up_ref[q, c], own_ref[q, c], down_ref[q, c]], axis=0)

    kappa = [whole(0, c) for c in range(TILES)]
    west, east = lane_shift(kappa, lane)
    for c in range(TILES):
        k, vx, vy = kappa[c], whole(1, c), whole(2, c)
        north, south = pltpu.roll(k, 1, 0), pltpu.roll(k, rows - 1, 0)
        fn, fs, fw, fe = (0.5 * (k + v) for v in (north, south, west[c], east[c]))
        inverse = 1.0 / (1.0 + TAU * (fn + fs + fw + fe))
        inverse = jnp.where(inside, inverse, 0.0)
        if c == 2:
            in_right = (lane < DEPTH) & (t < blocks - 1)
            in_left = (lane >= LANES - DEPTH) & (t > 0)
            inverse = jnp.where(in_right | in_left, inverse, 0.0)
        half = 0.5 * TAU
        values = (
            (TAU * fn + half * vy) * inverse,
            (TAU * fs - half * vy) * inverse,
            (TAU * fw + half * vx) * inverse,
            (TAU * fe - half * vx) * inverse,
            inverse,
        )
        for q, v in enumerate(values):
            for r in range(rows):
                out_ref[q, r, c] = jnp.broadcast_to(v[r : r + 1], (8, LANES))


def split(v):
    high = v.astype(BF16)
    return high, (v - high.astype(F32)).astype(BF16)


def relax(peers, up_ref, own_ref, down_ref, coef_ref, part_ref, change_ref, first_ref, field, start, right):
    n = own_ref.shape[0] // (TILES * DEPTH)
    lane = lax.broadcasted_iota(jnp.int32, (n, LANES), 1)
    weights = chebyshev_weights()
    rows = 3 * DEPTH

    def wide(q, r, c):
        v = coef_ref[q, r, c]
        return jnp.concatenate([v] * (n // 8), axis=0)

    for b, ref in enumerate((up_ref, own_ref, down_ref)):
        for r in range(DEPTH):
            for c in range(TILES):
                v = ref[pl.ds(c * DEPTH + r, n, stride=TILES * DEPTH), :]
                field[b * DEPTH + r, c] = v
                start[b * DEPTH + r, c] = v
                right[b * DEPTH + r, c] = v * wide(4, b * DEPTH + r, c)

    def sweep(k, weight):
        def one(r, north, here):
            south = [field[r + 1, c] for c in range(TILES)]
            west, east = lane_shift(here, lane)
            for c in range(TILES):
                pull = right[r, c] - here[c]
                pull += wide(0, r, c) * north[c] + wide(1, r, c) * south[c]
                pull += wide(2, r, c) * west[c] + wide(3, r, c) * east[c]
                field[r, c] = here[c] + weight * pull
            return here, south

        def two(i, carried):
            r = k + 2 * i
            north, here = carried
            north, here = one(r, north, here)
            return one(r + 1, north, here)

        lax.fori_loop(
            0,
            (rows - 2 * k) // 2,
            two,
            ([field[k - 1, c] for c in range(TILES)], [field[k, c] for c in range(TILES)]),
        )

    for step in range(STEPS):
        if step:
            done = step * SWEEPS

            def renew(r, carried):
                for c in range(TILES):
                    v = (4.0 * field[r, c] - start[r, c]) / 3.0
                    right[r, c] = v * wide(4, r, c)
                return carried

            lax.fori_loop(done + 1, rows - done - 1, renew, 0)
        for k in range(SWEEPS):
            sweep(step * SWEEPS + k + 1, weights[k])

    total = jnp.zeros((2 * n, 4 * n), F32)
    for r in range(DEPTH):
        s = jnp.concatenate([start[DEPTH + r, c] for c in range(2)], axis=1)
        e = jnp.concatenate([field[DEPTH + r, c] for c in range(2)], axis=1)
        change = e - s
        s_high, s_low = split(s)
        c_high, c_low = split(change)
        total += lax.dot_general(
            jnp.concatenate([s_high, s_low], axis=0),
            jnp.concatenate([s_high, c_high, s_low, c_low], axis=0),
            (((1,), (1,)), ((), ())),
            preferred_element_type=F32,
        )
        change_ref[:, r * 2 * LANES : (r + 1) * 2 * LANES] = jnp.concatenate([c_high, c_low], axis=0)
        first_ref[r : r + 1, :] = s[0:1]
    both = total[:n] + total[n:]
    both = both[:, : 2 * n] + both[:, 2 * n :]
    wide_both = jnp.concatenate([both] * 4, axis=1)
    lane = lax.broadcasted_iota(jnp.int32, (n, LANES), 1)
    row = lax.broadcasted_iota(jnp.int32, (n, LANES), 0)
    wide_both = jnp.where(lane // (2 * n) == row % 4, wide_both, 0.0)
    packed = [sum(wide_both[4 * q + p : 4 * q + p + 1] for p in range(4)) for q in range(n // 4)]
    packed = jnp.concatenate(packed, axis=0)
    for i in range(peers):
        part_ref[i] = packed


def add_up(peers, in_ref, out_ref):
    total = in_ref[0]
    for i in range(1, in_ref.shape[0]):
        total += in_ref[i]
    for i in range(peers):
        out_ref[i] = total


def correct(n, in_ref, change_ref, first_ref, out_ref):
    total = in_ref[0]
    for i in range(1, n):
        total += in_ref[i]
    lane = lax.broadcasted_iota(jnp.int32, (n, LANES), 1)
    row = lax.broadcasted_iota(jnp.int32, (n, LANES), 0)
    rows = jnp.concatenate([total[k // 4 : k // 4 + 1] for k in range(n)], axis=0)
    work = jnp.where(lane // (2 * n) == row % 4, rows, 0.0)
    work += pltpu.roll(work, 2 * n, 1)
    work += pltpu.roll(work, 4 * n, 1)
    for k in range(n):
        pivot = work[k : k + 1] / work[k : k + 1, k : k + 1]
        work = jnp.where(row == k, pivot, work - work[:, k : k + 1] * pivot)
    small = functools.partial(
        lax.dot_general, precision=lax.Precision.HIGHEST, preferred_element_type=F32
    )
    plain = (((1,), (0,)), ((), ()))
    lane_n = lax.broadcasted_iota(jnp.int32, (n, n), 1)
    row_n = lax.broadcasted_iota(jnp.int32, (n, n), 0)
    eye = jnp.where(lane_n == row_n, 1.0, 0.0).astype(F32)
    power = eye + small(work[:, n : 2 * n], eye, (((0,), (0,)), ((), ())))
    krylov = jnp.where((row_n == 0) & (lane_n == 0), 1.0, 0.0).astype(F32)
    step = 1
    while step < n:
        krylov += small(pltpu.roll(krylov, step, 0), power, plain)
        step *= 2
        if step < n:
            power = small(power, power, plain)
    mix = small(jnp.where(lane_n < row_n, 1.0, 0.0).astype(F32), krylov, plain)
    high, low = split(mix)
    left = jnp.concatenate(
        [jnp.concatenate([high, high], axis=1), jnp.concatenate([low, low], axis=1)], axis=0
    )
    for r in range(DEPTH):
        got = lax.dot_general(
            left,
            change_ref[:, r * 2 * LANES : (r + 1) * 2 * LANES],
            plain,
            preferred_element_type=F32,
        )
        got = got[:n] + got[n:] + first_ref[r : r + 1, :]
        for c in range(2):
            out_ref[pl.ds(c * DEPTH + r, n, stride=2 * DEPTH), :] = got[:, c * LANES : (c + 1) * LANES]


def spread(n, in_ref, out_ref):
    for i in range(2 * n):
        out_ref[:, i * LANES : (i + 1) * LANES] = in_ref[i]


def per_device(starts, kappa, velocity_x, velocity_y):
    n, slabs = lax.axis_size("tm"), lax.axis_size("space")
    pos = jnp.stack([lax.axis_index("tm"), lax.axis_index("space")]).astype(jnp.int32)
    shape = jax.ShapeDtypeStruct
    down = [(i, i + 1) for i in range(slabs - 1)]
    up = [(i + 1, i) for i in range(slabs - 1)]

    def exchange(v, axis):
        return lax.all_to_all(v, axis, 0, 0, tiled=True)

    blocks, coefs = call(
        functools.partial(pack, n),
        [shape((n, TILES, DEPTH, LANES), F32), shape((3, TILES, DEPTH, LANES), F32)],
        smem=1,
        n_in=5,
    )(pos, starts[0], kappa, velocity_x, velocity_y)
    own = exchange(blocks, "tm")
    above, below = lax.ppermute(coefs, "space", down), lax.ppermute(coefs, "space", up)
    (table,) = call(
        functools.partial(stencil, n, slabs),
        [shape((5, 3 * DEPTH, TILES, 8, LANES), F32)],
        smem=1,
        n_in=4,
    )(pos, above, coefs, below)
    own_above, own_below = lax.ppermute(own, "space", down), lax.ppermute(own, "space", up)
    flat = (n * TILES * DEPTH, LANES)
    grid = pltpu.VMEM((3 * DEPTH, TILES, n, LANES), F32)
    part, change, first = call(
        functools.partial(relax, slabs),
        [
            shape((slabs, n // 4, LANES), F32),
            shape((2 * n, DEPTH * 2 * LANES), BF16),
            shape((DEPTH, 2 * LANES), F32),
        ],
        scratch=[grid, grid, grid],
        n_in=4,
    )(own_above.reshape(flat), own.reshape(flat), own_below.reshape(flat), table)
    (part,) = call(functools.partial(add_up, n), [shape((n, n // 4, LANES), F32)])(exchange(part, "space"))
    (result,) = call(
        functools.partial(correct, n),
        [shape((n * 2 * DEPTH, LANES), F32)],
        n_in=3,
    )(exchange(part, "tm"), change, first)
    result = exchange(result.reshape(n, 2, DEPTH, LANES), "tm")
    (result,) = call(functools.partial(spread, n), [shape((DEPTH, n * 2 * LANES), F32)])(
        result.reshape(2 * n, DEPTH, LANES)
    )
    return result[None]


def solution(mesh):
    in_specs = (P("tm", "space", None), P("space", None), P("space", None), P("space", None))
    out_specs = P("tm", "space", None)
    return jax.shard_map(
        per_device, mesh=mesh, in_specs=in_specs, out_specs=out_specs, check_vma=False
    )
```

```python
import functools
import math

import jax
import jax.numpy as jnp
from jax import lax
from jax.experimental import pallas as pl
from jax.experimental.pallas import tpu as pltpu
from jax.sharding import PartitionSpec as P

STEPS = 2
SWEEPS = 8
TAU = 0.4
LANES = 128
DEPTH = STEPS * SWEEPS
TILES = 3
UNROLL = 16
VMEM = 48 * 2**20

F32 = jnp.float32
BF16 = jnp.bfloat16


def chebyshev_weights():
    return [
        1.0 / (1.0 - 0.8 * math.cos(math.pi * (2 * k + 1) / (2.0 * SWEEPS)))
        for k in range(SWEEPS)
    ]


def call(body, outs, scratch=(), smem=0, hbm=0, n_in=1):
    specs = [pl.BlockSpec(memory_space=pltpu.SMEM)] * smem
    specs += [pl.BlockSpec(memory_space=pltpu.HBM)] * hbm
    specs += [pl.BlockSpec(memory_space=pltpu.VMEM)] * (n_in - smem - hbm)
    return pl.pallas_call(
        body,
        out_shape=outs,
        in_specs=specs,
        out_specs=[pl.BlockSpec(memory_space=pltpu.VMEM)] * len(outs),
        scratch_shapes=list(scratch),
        compiler_params=pltpu.CompilerParams(vmem_limit_bytes=VMEM),
    )


BLOCK = 2 * DEPTH + 8


def fold(rim):
    rim = pltpu.roll(rim, DEPTH, 1)
    return rim[:8] + pltpu.roll(rim[8:], LANES // 2, 1)


def unfold(folded, half, lane):
    rim = pltpu.roll(folded, (LANES - DEPTH - half * (LANES // 2)) % LANES, 1)
    return jnp.where((lane < DEPTH) | (lane >= LANES - DEPTH), rim, 0.0)


def pack(blocks, pos_ref, x_hbm, kappa_hbm, vx_hbm, vy_hbm, a_ref, c_ref, x_ref, f_ref, x_sem, f_sem):
    lane = lax.broadcasted_iota(jnp.int32, (DEPTH, LANES), 1)
    zero = jnp.zeros((DEPTH, LANES), F32)
    t = pos_ref[0]
    tiles = 2 * blocks
    chunks = x_sem.shape[0]
    width = tiles * LANES // chunks
    copies = [
        pltpu.make_async_copy(
            x_hbm.at[:, pl.ds(i * width, width)], x_ref.at[:, pl.ds(i * width, width)], x_sem.at[i]
        )
        for i in range(chunks)
    ]
    first = jnp.minimum(jnp.maximum(2 * t - 1, 0), tiles - 4)
    begin = pl.multiple_of(first * LANES, LANES)
    small = [
        pltpu.make_async_copy(ref.at[:, pl.ds(begin, 4 * LANES)], f_ref.at[q], f_sem.at[q])
        for q, ref in enumerate((kappa_hbm, vx_hbm, vy_hbm))
    ]
    for copy in copies + small:
        copy.start()

    def put(ref, i, one, two, left, right):
        rim = jnp.where(lane < DEPTH, right, jnp.where(lane >= LANES - DEPTH, left, 0.0))
        ref[i, :DEPTH] = one
        ref[i, DEPTH : 2 * DEPTH] = two
        ref[i, 2 * DEPTH :] = fold(rim)

    def tile(i):
        return x_ref[:, i * LANES : (i + 1) * LANES] if 0 <= i < tiles else zero

    for copy in copies:
        copy.wait()
    for i in range(blocks):
        put(a_ref, i, *(tile(2 * i + j) for j in (0, 1, -1, 2)))
    for copy in small:
        copy.wait()
    for q in range(3):

        def at(i):
            i = jnp.minimum(jnp.maximum(i - first, 0), 3)
            return f_ref[q, :, pl.ds(pl.multiple_of(i * LANES, LANES), LANES)]

        left = jnp.where(t > 0, at(2 * t - 1), 0.0)
        right = jnp.where(t < blocks - 1, at(2 * t + 2), 0.0)
        put(c_ref, q, at(2 * t), at(2 * t + 1), left, right)


def lane_shift(tiles, lane):
    back = [pltpu.roll(v, 1, 1) for v in tiles]
    fore = [pltpu.roll(v, LANES - 1, 1) for v in tiles]
    west = [jnp.where(lane == 0, back[(c + 2) % 3], back[c]) for c in range(3)]
    east = [jnp.where(lane == LANES - 1, fore[(c + 1) % 3], fore[c]) for c in range(3)]
    return west, east


def stencil(blocks, slabs, n, pos_ref, refs, out_ref):
    rows = 3 * DEPTH
    t, s = pos_ref[0], pos_ref[1]
    lane = lax.broadcasted_iota(jnp.int32, (rows, LANES), 1)
    lane8 = lax.broadcasted_iota(jnp.int32, (8, LANES), 1)
    row = lax.broadcasted_iota(jnp.int32, (rows, LANES), 0) + (s - 1) * DEPTH
    inside = (row >= 0) & (row < slabs * DEPTH)

    def whole(q, c):
        base = (n + q) * BLOCK + c * DEPTH
        if c < 2:
            return jnp.concatenate([ref[base : base + DEPTH, :] for ref in refs], axis=0)
        return jnp.concatenate(
            [unfold(ref[base : base + 8, :], half, lane8) for ref in refs for half in range(2)], axis=0
        )

    kappa = [whole(0, c) for c in range(TILES)]
    west, east = lane_shift(kappa, lane)
    for c in range(TILES):
        k, vx, vy = kappa[c], whole(1, c), whole(2, c)
        north, south = pltpu.roll(k, 1, 0), pltpu.roll(k, rows - 1, 0)
        fn, fs, fw, fe = (0.5 * (k + v) for v in (north, south, west[c], east[c]))
        inverse = 1.0 / (1.0 + TAU * (fn + fs + fw + fe))
        inverse = jnp.where(inside, inverse, 0.0)
        if c == 2:
            in_right = (lane < DEPTH) & (t < blocks - 1)
            in_left = (lane >= LANES - DEPTH) & (t > 0)
            inverse = jnp.where(in_right | in_left, inverse, 0.0)
        half = 0.5 * TAU
        values = (
            (TAU * fn + half * vy) * inverse,
            (TAU * fs - half * vy) * inverse,
            (TAU * fw + half * vx) * inverse,
            (TAU * fe - half * vx) * inverse,
            inverse,
        )
        for q, v in enumerate(values):
            for r in range(rows):
                out_ref[q, r, c] = jnp.broadcast_to(v[r : r + 1], (8, LANES))


def split(v):
    high = v.astype(BF16)
    return high, (v - high.astype(F32)).astype(BF16)


def relax(n, slabs, pos_ref, up_ref, own_ref, down_ref, part_ref, change_ref, first_ref, coef_ref, field, start, right):
    refs = (up_ref, own_ref, down_ref)
    stencil(n, slabs, n, pos_ref, refs, coef_ref)
    lane = lax.broadcasted_iota(jnp.int32, (n, LANES), 1)
    weights = chebyshev_weights()
    rows = 3 * DEPTH

    def wide(q, r, c):
        v = coef_ref[q, r, c]
        return jnp.concatenate([v] * (n // 8), axis=0)

    def begin(r, c, v):
        field[r, c] = v
        start[r, c] = v
        right[r, c] = v * wide(4, r, c)

    for b, ref in enumerate(refs):
        for c in range(2):
            for r in range(DEPTH):
                begin(b * DEPTH + r, c, ref[pl.ds(c * DEPTH + r, n, stride=BLOCK), :])
        for r in range(8):
            folded = ref[pl.ds(2 * DEPTH + r, n, stride=BLOCK), :]
            for half in range(2):
                begin(b * DEPTH + half * 8 + r, 2, unfold(folded, half, lane))

    def sweep(k, weight):
        def one(r, north, here):
            south = [field[r + 1, c] for c in range(TILES)]
            west, east = lane_shift(here, lane)
            for c in range(TILES):
                pull = right[r, c] - here[c]
                pull += wide(0, r, c) * north[c] + wide(1, r, c) * south[c]
                pull += wide(2, r, c) * west[c] + wide(3, r, c) * east[c]
                field[r, c] = here[c] + weight * pull
            return here, south

        def many(i, carried):
            for u in range(UNROLL):
                carried = one(k + UNROLL * i + u, *carried)
            return carried

        count = rows - 2 * k
        carried = lax.fori_loop(
            0,
            count // UNROLL,
            many,
            ([field[k - 1, c] for c in range(TILES)], [field[k, c] for c in range(TILES)]),
        )
        for r in range(k + count // UNROLL * UNROLL, k + count):
            carried = one(r, *carried)

    for step in range(STEPS):
        if step:
            done = step * SWEEPS

            def renew(r, carried):
                for c in range(TILES):
                    v = (4.0 * field[r, c] - start[r, c]) / 3.0
                    right[r, c] = v * wide(4, r, c)
                return carried

            lax.fori_loop(done + 1, rows - done - 1, renew, 0)
        for k in range(SWEEPS):
            sweep(step * SWEEPS + k + 1, weights[k])

    total = jnp.zeros((2 * n, 4 * n), F32)
    for r in range(DEPTH):
        s = jnp.concatenate([start[DEPTH + r, c] for c in range(2)], axis=1)
        e = jnp.concatenate([field[DEPTH + r, c] for c in range(2)], axis=1)
        change = e - s
        s_high, s_low = split(s)
        c_high, c_low = split(change)
        total += lax.dot_general(
            jnp.concatenate([s_high, s_low], axis=0),
            jnp.concatenate([s_high, c_high, s_low, c_low], axis=0),
            (((1,), (1,)), ((), ())),
            preferred_element_type=F32,
        )
        change_ref[:, r * 2 * LANES : (r + 1) * 2 * LANES] = jnp.concatenate([c_high, c_low], axis=0)
        first_ref[r : r + 1, :] = s[0:1]
    both = total[:n] + total[n:]
    both = both[:, : 2 * n] + both[:, 2 * n :]
    wide_both = jnp.concatenate([both] * 4, axis=1)
    lane = lax.broadcasted_iota(jnp.int32, (n, LANES), 1)
    row = lax.broadcasted_iota(jnp.int32, (n, LANES), 0)
    wide_both = jnp.where(lane // (2 * n) == row % 4, wide_both, 0.0)
    packed = [sum(wide_both[4 * q + p : 4 * q + p + 1] for p in range(4)) for q in range(n // 4)]
    packed = jnp.concatenate(packed, axis=0)
    for i in range(slabs):
        part_ref[i] = packed


def add_up(peers, in_ref, out_ref):
    total = in_ref[0]
    for i in range(1, in_ref.shape[0]):
        total += in_ref[i]
    for i in range(peers):
        out_ref[i] = total


def correct(n, in_ref, change_ref, first_ref, out_ref):
    total = in_ref[0]
    for i in range(1, n):
        total += in_ref[i]
    lane = lax.broadcasted_iota(jnp.int32, (n, LANES), 1)
    row = lax.broadcasted_iota(jnp.int32, (n, LANES), 0)
    rows = jnp.concatenate([total[k // 4 : k // 4 + 1] for k in range(n)], axis=0)
    work = jnp.where(lane // (2 * n) == row % 4, rows, 0.0)
    work += pltpu.roll(work, 2 * n, 1)
    work += pltpu.roll(work, 4 * n, 1)
    for k in range(n):
        pivot = work[k : k + 1] / work[k : k + 1, k : k + 1]
        work = jnp.where(row == k, pivot, work - work[:, k : k + 1] * pivot)
    small = functools.partial(
        lax.dot_general, precision=lax.Precision.HIGHEST, preferred_element_type=F32
    )
    plain = (((1,), (0,)), ((), ()))
    lane_n = lax.broadcasted_iota(jnp.int32, (n, n), 1)
    row_n = lax.broadcasted_iota(jnp.int32, (n, n), 0)
    eye = jnp.where(lane_n == row_n, 1.0, 0.0).astype(F32)
    power = eye + small(work[:, n : 2 * n], eye, (((0,), (0,)), ((), ())))
    krylov = jnp.where((row_n == 0) & (lane_n == 0), 1.0, 0.0).astype(F32)
    step = 1
    while step < n:
        krylov += small(pltpu.roll(krylov, step, 0), power, plain)
        step *= 2
        if step < n:
            power = small(power, power, plain)
    mix = small(jnp.where(lane_n < row_n, 1.0, 0.0).astype(F32), krylov, plain)
    high, low = split(mix)
    left = jnp.concatenate(
        [jnp.concatenate([high, high], axis=1), jnp.concatenate([low, low], axis=1)], axis=0
    )
    for r in range(DEPTH):
        got = lax.dot_general(
            left,
            change_ref[:, r * 2 * LANES : (r + 1) * 2 * LANES],
            plain,
            preferred_element_type=F32,
        )
        got = got[:n] + got[n:] + first_ref[r : r + 1, :]
        for c in range(2):
            out_ref[pl.ds(c * DEPTH + r, n, stride=2 * DEPTH), :] = got[:, c * LANES : (c + 1) * LANES]


def spread(n, in_ref, out_ref):
    for i in range(2 * n):
        out_ref[:, i * LANES : (i + 1) * LANES] = in_ref[i]


def per_device(starts, kappa, velocity_x, velocity_y):
    n, slabs = lax.axis_size("tm"), lax.axis_size("space")
    pos = jnp.stack([lax.axis_index("tm"), lax.axis_index("space")]).astype(jnp.int32)
    shape = jax.ShapeDtypeStruct
    down = [(i, i + 1) for i in range(slabs - 1)]
    up = [(i + 1, i) for i in range(slabs - 1)]

    def exchange(v, axis):
        return lax.all_to_all(v, axis, 0, 0, tiled=True)

    blocks, coefs = call(
        functools.partial(pack, n),
        [shape((n, BLOCK, LANES), F32), shape((3, BLOCK, LANES), F32)],
        scratch=[
            pltpu.VMEM(starts.shape[1:], F32),
            pltpu.VMEM((3, DEPTH, 4 * LANES), F32),
            pltpu.SemaphoreType.DMA((4,)),
            pltpu.SemaphoreType.DMA((3,)),
        ],
        smem=1,
        hbm=4,
        n_in=5,
    )(pos, starts[0], kappa, velocity_x, velocity_y)
    own = jnp.concatenate([exchange(blocks, "tm"), coefs], axis=0).reshape((n + 3) * BLOCK, LANES)
    above, below = lax.ppermute(own, "space", down), lax.ppermute(own, "space", up)
    grid = pltpu.VMEM((3 * DEPTH, TILES, n, LANES), F32)
    part, change, first = call(
        functools.partial(relax, n, slabs),
        [
            shape((slabs, n // 4, LANES), F32),
            shape((2 * n, DEPTH * 2 * LANES), BF16),
            shape((DEPTH, 2 * LANES), F32),
        ],
        scratch=[pltpu.VMEM((5, 3 * DEPTH, TILES, 8, LANES), F32), grid, grid, grid],
        smem=1,
        n_in=4,
    )(pos, above, own, below)
    (part,) = call(functools.partial(add_up, n), [shape((n, n // 4, LANES), F32)])(exchange(part, "space"))
    (result,) = call(
        functools.partial(correct, n),
        [shape((n * 2 * DEPTH, LANES), F32)],
        n_in=3,
    )(exchange(part, "tm"), change, first)
    result = exchange(result.reshape(n, 2, DEPTH, LANES), "tm")
    (result,) = call(functools.partial(spread, n), [shape((DEPTH, n * 2 * LANES), F32)])(
        result.reshape(2 * n, DEPTH, LANES)
    )
    return result[None]


def solution(mesh):
    in_specs = (P("tm", "space", None), P("space", None), P("space", None), P("space", None))
    out_specs = P("tm", "space", None)
    return jax.shard_map(
        per_device, mesh=mesh, in_specs=in_specs, out_specs=out_specs, check_vma=False
    )
```

```python
import functools
import math

import jax
import jax.numpy as jnp
from jax import lax
from jax.experimental import pallas as pl
from jax.experimental.pallas import tpu as pltpu
from jax.sharding import PartitionSpec as P

STEPS = 2
SWEEPS = 8
TAU = 0.4
LANES = 128
DEPTH = STEPS * SWEEPS
TILES = 3
VMEM = 48 * 2**20

F32 = jnp.float32
BF16 = jnp.bfloat16


def chebyshev_weights():
    return [
        1.0 / (1.0 - 0.8 * math.cos(math.pi * (2 * k + 1) / (2.0 * SWEEPS)))
        for k in range(SWEEPS)
    ]


def call(body, outs, scratch=(), smem=0, hbm=0, n_in=1):
    specs = [pl.BlockSpec(memory_space=pltpu.SMEM)] * smem
    specs += [pl.BlockSpec(memory_space=pltpu.HBM)] * hbm
    specs += [pl.BlockSpec(memory_space=pltpu.VMEM)] * (n_in - smem - hbm)
    return pl.pallas_call(
        body,
        out_shape=outs,
        in_specs=specs,
        out_specs=[pl.BlockSpec(memory_space=pltpu.VMEM)] * len(outs),
        scratch_shapes=list(scratch),
        compiler_params=pltpu.CompilerParams(vmem_limit_bytes=VMEM),
    )


BLOCK = 2 * DEPTH + 8


def fold(rim):
    rim = pltpu.roll(rim, DEPTH, 1)
    return rim[:8] + pltpu.roll(rim[8:], LANES // 2, 1)


def unfold(folded, half, lane):
    rim = pltpu.roll(folded, (LANES - DEPTH - half * (LANES // 2)) % LANES, 1)
    return jnp.where((lane < DEPTH) | (lane >= LANES - DEPTH), rim, 0.0)


def pack(blocks, pos_ref, x_hbm, kappa_hbm, vx_hbm, vy_hbm, a_ref, c_ref, x_ref, f_ref, x_sem, f_sem):
    lane = lax.broadcasted_iota(jnp.int32, (DEPTH, LANES), 1)
    zero = jnp.zeros((DEPTH, LANES), F32)
    t = pos_ref[0]
    tiles = 2 * blocks
    chunks = x_sem.shape[0]
    width = tiles * LANES // chunks
    copies = [
        pltpu.make_async_copy(
            x_hbm.at[:, pl.ds(i * width, width)], x_ref.at[:, pl.ds(i * width, width)], x_sem.at[i]
        )
        for i in range(chunks)
    ]
    first = jnp.minimum(jnp.maximum(2 * t - 1, 0), tiles - 4)
    begin = pl.multiple_of(first * LANES, LANES)
    small = [
        pltpu.make_async_copy(ref.at[:, pl.ds(begin, 4 * LANES)], f_ref.at[q], f_sem.at[q])
        for q, ref in enumerate((kappa_hbm, vx_hbm, vy_hbm))
    ]
    for copy in copies + small:
        copy.start()

    def put(ref, i, one, two, left, right):
        rim = jnp.where(lane < DEPTH, right, jnp.where(lane >= LANES - DEPTH, left, 0.0))
        ref[i, :DEPTH] = one
        ref[i, DEPTH : 2 * DEPTH] = two
        ref[i, 2 * DEPTH :] = fold(rim)

    def tile(i):
        return x_ref[:, i * LANES : (i + 1) * LANES] if 0 <= i < tiles else zero

    for copy in copies:
        copy.wait()
    for i in range(blocks):
        put(a_ref, i, *(tile(2 * i + j) for j in (0, 1, -1, 2)))
    for copy in small:
        copy.wait()
    for q in range(3):

        def at(i):
            i = jnp.minimum(jnp.maximum(i - first, 0), 3)
            return f_ref[q, :, pl.ds(pl.multiple_of(i * LANES, LANES), LANES)]

        left = jnp.where(t > 0, at(2 * t - 1), 0.0)
        right = jnp.where(t < blocks - 1, at(2 * t + 2), 0.0)
        put(c_ref, q, at(2 * t), at(2 * t + 1), left, right)


def lane_shift(tiles, lane):
    back = [pltpu.roll(v, 1, 1) for v in tiles]
    fore = [pltpu.roll(v, LANES - 1, 1) for v in tiles]
    west = [jnp.where(lane == 0, back[(c + 2) % 3], back[c]) for c in range(3)]
    east = [jnp.where(lane == LANES - 1, fore[(c + 1) % 3], fore[c]) for c in range(3)]
    return west, east


def reader(pos_ref, own_ref, chip_ref, link_ref):
    odd = lax.rem(pos_ref[1], 2) == 1

    def read(b, *at):
        if b == 1:
            return own_ref[at]
        pair = (chip_ref[at], link_ref[at])
        return jnp.where(odd, *(pair if b == 0 else pair[::-1]))

    return read


def stencil(blocks, slabs, pos_ref, own_ref, chip_ref, link_ref, out_ref):
    rows = 3 * DEPTH
    t, s = pos_ref[0], pos_ref[1]
    lane = lax.broadcasted_iota(jnp.int32, (rows, LANES), 1)
    lane8 = lax.broadcasted_iota(jnp.int32, (8, LANES), 1)
    row = lax.broadcasted_iota(jnp.int32, (rows, LANES), 0) + (s - 1) * DEPTH
    inside = (row >= 0) & (row < slabs * DEPTH)

    read = reader(pos_ref, own_ref, chip_ref, link_ref)

    def whole(q, c):
        base = c * DEPTH
        if c < 2:
            return jnp.concatenate([read(b, q, pl.ds(base, DEPTH)) for b in range(3)], axis=0)
        return jnp.concatenate(
            [unfold(read(b, q, pl.ds(base, 8)), half, lane8) for b in range(3) for half in range(2)], axis=0
        )

    kappa = [whole(0, c) for c in range(TILES)]
    west, east = lane_shift(kappa, lane)
    for c in range(TILES):
        k, vx, vy = kappa[c], whole(1, c), whole(2, c)
        north, south = pltpu.roll(k, 1, 0), pltpu.roll(k, rows - 1, 0)
        fn, fs, fw, fe = (0.5 * (k + v) for v in (north, south, west[c], east[c]))
        inverse = 1.0 / (1.0 + TAU * (fn + fs + fw + fe))
        inverse = jnp.where(inside, inverse, 0.0)
        if c == 2:
            in_right = (lane < DEPTH) & (t < blocks - 1)
            in_left = (lane >= LANES - DEPTH) & (t > 0)
            inverse = jnp.where(in_right | in_left, inverse, 0.0)
        half = 0.5 * TAU
        values = (
            (TAU * fn + half * vy) * inverse,
            (TAU * fs - half * vy) * inverse,
            (TAU * fw + half * vx) * inverse,
            (TAU * fe - half * vx) * inverse,
            inverse,
        )
        for q, v in enumerate(values):
            for r in range(rows):
                out_ref[q, r, c] = jnp.broadcast_to(v[r : r + 1], (8, LANES))


def split(v):
    high = v.astype(BF16)
    return high, (v - high.astype(F32)).astype(BF16)


def relax(n, slabs, pos_ref, own_ref, chip_ref, link_ref, coef_ref, part_ref, change_ref, first_ref, field, start, right):
    lane = lax.broadcasted_iota(jnp.int32, (n, LANES), 1)
    weights = chebyshev_weights()
    rows = 3 * DEPTH

    def wide(q, r, c):
        v = coef_ref[q, r, c]
        return jnp.concatenate([v] * (n // 8), axis=0)

    def begin(r, c, v):
        field[r, c] = v
        start[r, c] = v
        right[r, c] = v * wide(4, r, c)

    def slab(b, ref):
        for c in range(2):
            for r in range(DEPTH):
                begin(b * DEPTH + r, c, ref[pl.ds(c * DEPTH + r, n, stride=BLOCK), :])
        for r in range(8):
            folded = ref[pl.ds(2 * DEPTH + r, n, stride=BLOCK), :]
            for half in range(2):
                begin(b * DEPTH + half * 8 + r, 2, unfold(folded, half, lane))

    odd = lax.rem(pos_ref[1], 2) == 1
    slab(1, own_ref)

    @pl.when(odd)
    def _():
        slab(0, chip_ref)
        slab(2, link_ref)

    @pl.when(jnp.logical_not(odd))
    def _():
        slab(0, link_ref)
        slab(2, chip_ref)

    def sweep(k, weight):
        def one(r, north, here):
            south = [field[r + 1, c] for c in range(TILES)]
            west, east = lane_shift(here, lane)
            for c in range(TILES):
                pull = right[r, c] - here[c]
                pull += wide(0, r, c) * north[c] + wide(1, r, c) * south[c]
                pull += wide(2, r, c) * west[c] + wide(3, r, c) * east[c]
                field[r, c] = here[c] + weight * pull
            return here, south

        carried = ([field[k - 1, c] for c in range(TILES)], [field[k, c] for c in range(TILES)])
        for r in range(k, rows - k):
            carried = one(r, *carried)

    for step in range(STEPS):
        if step:
            done = step * SWEEPS

            for r in range(done + 1, rows - done - 1):
                for c in range(TILES):
                    v = (4.0 * field[r, c] - start[r, c]) / 3.0
                    right[r, c] = v * wide(4, r, c)
        for k in range(SWEEPS):
            sweep(step * SWEEPS + k + 1, weights[k])

    total = jnp.zeros((2 * n, 4 * n), F32)
    for r in range(DEPTH):
        s = jnp.concatenate([start[DEPTH + r, c] for c in range(2)], axis=1)
        e = jnp.concatenate([field[DEPTH + r, c] for c in range(2)], axis=1)
        change = e - s
        s_high, s_low = split(s)
        c_high, c_low = split(change)
        total += lax.dot_general(
            jnp.concatenate([s_high, s_low], axis=0),
            jnp.concatenate([s_high, c_high, s_low, c_low], axis=0),
            (((1,), (1,)), ((), ())),
            preferred_element_type=F32,
        )
        change_ref[:, r * 2 * LANES : (r + 1) * 2 * LANES] = jnp.concatenate([c_high, c_low], axis=0)
        first_ref[r : r + 1, :] = s[0:1]
    both = total[:n] + total[n:]
    both = both[:, : 2 * n] + both[:, 2 * n :]
    wide_both = jnp.concatenate([both] * 4, axis=1)
    lane = lax.broadcasted_iota(jnp.int32, (n, LANES), 1)
    row = lax.broadcasted_iota(jnp.int32, (n, LANES), 0)
    wide_both = jnp.where(lane // (2 * n) == row % 4, wide_both, 0.0)
    packed = [sum(wide_both[4 * q + p : 4 * q + p + 1] for p in range(4)) for q in range(n // 4)]
    packed = jnp.concatenate(packed, axis=0)
    for i in range(slabs):
        part_ref[i] = packed


def add_up(peers, in_ref, out_ref):
    total = in_ref[0]
    for i in range(1, in_ref.shape[0]):
        total += in_ref[i]
    for i in range(peers):
        out_ref[i] = total


def correct(n, in_ref, change_ref, first_ref, out_ref):
    total = in_ref[0]
    for i in range(1, n):
        total += in_ref[i]
    lane = lax.broadcasted_iota(jnp.int32, (n, LANES), 1)
    row = lax.broadcasted_iota(jnp.int32, (n, LANES), 0)
    rows = jnp.concatenate([total[k // 4 : k // 4 + 1] for k in range(n)], axis=0)
    work = jnp.where(lane // (2 * n) == row % 4, rows, 0.0)
    work += pltpu.roll(work, 2 * n, 1)
    work += pltpu.roll(work, 4 * n, 1)
    for k in range(n):
        pivot = work[k : k + 1] / work[k : k + 1, k : k + 1]
        work = jnp.where(row == k, pivot, work - work[:, k : k + 1] * pivot)
    small = functools.partial(
        lax.dot_general, precision=lax.Precision.HIGHEST, preferred_element_type=F32
    )
    plain = (((1,), (0,)), ((), ()))
    across = (((1,), (1,)), ((), ()))
    power = jnp.where(lane < n, pltpu.roll(work, LANES - n, 1), 0.0)
    power += jnp.where((lane == row) | ((lane == n) & (row == 0)), 1.0, 0.0)
    last = jnp.where((lane == n) & (row == 0), 1.0, 0.0)
    power = jnp.concatenate([power, last], axis=0)[:, : 2 * n]
    states = last[:, : 2 * n]
    step = 1
    while step < n:
        states += small(pltpu.roll(states, step, 0), power, across)
        step *= 2
        if step < n:
            power = small(power, power, plain)
    mix = states[:, :n]
    high, low = split(mix)
    left = jnp.concatenate(
        [jnp.concatenate([high, high], axis=1), jnp.concatenate([low, low], axis=1)], axis=0
    )
    for r in range(DEPTH):
        got = lax.dot_general(
            left,
            change_ref[:, r * 2 * LANES : (r + 1) * 2 * LANES],
            plain,
            preferred_element_type=F32,
        )
        got = got[:n] + got[n:] + first_ref[r : r + 1, :]
        for c in range(2):
            out_ref[pl.ds(c * DEPTH + r, n, stride=2 * DEPTH), :] = got[:, c * LANES : (c + 1) * LANES]


def spread(n, in_ref, out_ref):
    for i in range(2 * n):
        out_ref[:, i * LANES : (i + 1) * LANES] = in_ref[i]


def per_device(starts, kappa, velocity_x, velocity_y):
    n, slabs = lax.axis_size("tm"), lax.axis_size("space")
    pos = jnp.stack([lax.axis_index("tm"), lax.axis_index("space")]).astype(jnp.int32)
    shape = jax.ShapeDtypeStruct
    chip = [(i, i ^ 1) for i in range(slabs)]
    link = [(i, j) for i in range(slabs) if 0 <= (j := i + (1 if i % 2 else -1)) < slabs]

    def exchange(v, axis):
        return lax.all_to_all(v, axis, 0, 0, tiled=True)

    def neighbours(v):
        return lax.ppermute(v, "space", chip), lax.ppermute(v, "space", link)

    blocks, coefs = call(
        functools.partial(pack, n),
        [shape((n, BLOCK, LANES), F32), shape((3, BLOCK, LANES), F32)],
        scratch=[
            pltpu.VMEM(starts.shape[1:], F32),
            pltpu.VMEM((3, DEPTH, 4 * LANES), F32),
            pltpu.SemaphoreType.DMA((4,)),
            pltpu.SemaphoreType.DMA((3,)),
        ],
        smem=1,
        hbm=4,
        n_in=5,
    )(pos, *(pltpu.with_memory_space_constraint(v, pltpu.HBM) for v in (starts[0], kappa, velocity_x, velocity_y)))
    own = exchange(blocks, "tm").reshape(n * BLOCK, LANES)
    coef_chip, coef_link = neighbours(coefs)
    (table,) = call(
        functools.partial(stencil, n, slabs),
        [shape((5, 3 * DEPTH, TILES, 8, LANES), F32)],
        smem=1,
        n_in=4,
    )(pos, coefs, coef_chip, coef_link)
    own, table = lax.optimization_barrier((own, table))
    own_chip, own_link = neighbours(own)
    grid = pltpu.VMEM((3 * DEPTH, TILES, n, LANES), F32)
    part, change, first = call(
        functools.partial(relax, n, slabs),
        [
            shape((slabs, n // 4, LANES), F32),
            shape((2 * n, DEPTH * 2 * LANES), BF16),
            shape((DEPTH, 2 * LANES), F32),
        ],
        scratch=[grid, grid, grid],
        smem=1,
        n_in=5,
    )(pos, own, own_chip, own_link, table)
    (part,) = call(functools.partial(add_up, n), [shape((n, n // 4, LANES), F32)])(exchange(part, "space"))
    (result,) = call(
        functools.partial(correct, n),
        [shape((n * 2 * DEPTH, LANES), F32)],
        n_in=3,
    )(exchange(part, "tm"), change, first)
    result = exchange(result.reshape(n, 2, DEPTH, LANES), "tm")
    (result,) = call(functools.partial(spread, n), [shape((DEPTH, n * 2 * LANES), F32)])(
        result.reshape(2 * n, DEPTH, LANES)
    )
    return result[None]


def solution(mesh):
    in_specs = (P("tm", "space", None), P("space", None), P("space", None), P("space", None))
    out_specs = P("tm", "space", None)
    return jax.shard_map(
        per_device, mesh=mesh, in_specs=in_specs, out_specs=out_specs, check_vma=False
    )
```

```python
import functools
import math

import jax
import jax.numpy as jnp
from jax import lax
from jax.experimental import pallas as pl
from jax.experimental.pallas import tpu as pltpu
from jax.sharding import PartitionSpec as P

STEPS = 2
SWEEPS = 8
TAU = 0.4
LANES = 128
DEPTH = STEPS * SWEEPS
TILES = 3
VMEM = 48 * 2**20

F32 = jnp.float32
BF16 = jnp.bfloat16


def chebyshev_weights():
    return [
        1.0 / (1.0 - 0.8 * math.cos(math.pi * (2 * k + 1) / (2.0 * SWEEPS)))
        for k in range(SWEEPS)
    ]


def call(body, outs, scratch=(), smem=0, hbm=0, n_in=1):
    specs = [pl.BlockSpec(memory_space=pltpu.SMEM)] * smem
    specs += [pl.BlockSpec(memory_space=pltpu.HBM)] * hbm
    specs += [pl.BlockSpec(memory_space=pltpu.VMEM)] * (n_in - smem - hbm)
    return pl.pallas_call(
        body,
        out_shape=outs,
        in_specs=specs,
        out_specs=[pl.BlockSpec(memory_space=pltpu.VMEM)] * len(outs),
        scratch_shapes=list(scratch),
        compiler_params=pltpu.CompilerParams(vmem_limit_bytes=VMEM),
    )


BLOCK = 2 * DEPTH + 4
COEF = 2 * DEPTH + 8


def fold(rim, rows):
    rim = pltpu.roll(rim, DEPTH, 1)
    shift = LANES // 2
    while rim.shape[0] > rows:
        half = rim.shape[0] // 2
        rim = rim[:half] + pltpu.roll(rim[half:], shift, 1)
        shift //= 2
    return rim


def unfold(folded, shift, lane):
    rim = pltpu.roll(folded, (LANES - DEPTH - shift) % LANES, 1)
    return jnp.where((lane < DEPTH) | (lane >= LANES - DEPTH), rim, 0.0)


def rim(left, right, rows):
    lane = lax.broadcasted_iota(jnp.int32, left.shape, 1)
    return fold(jnp.where(lane < DEPTH, right, jnp.where(lane >= LANES - DEPTH, left, 0.0)), rows)


def pack(blocks, x_ref, a_ref):
    def tile(j):
        inside = 0 <= j < 2 * blocks
        return x_ref[:, j * LANES : (j + 1) * LANES] if inside else jnp.zeros((DEPTH, LANES), F32)

    for k in range(blocks):
        a_ref[k * BLOCK : k * BLOCK + DEPTH] = tile(2 * k)
        a_ref[k * BLOCK + DEPTH : k * BLOCK + 2 * DEPTH] = tile(2 * k + 1)
        a_ref[k * BLOCK + 2 * DEPTH : (k + 1) * BLOCK] = rim(tile(2 * k - 1), tile(2 * k + 2), 4)


def pack_coefficients(blocks, pos_ref, kappa_hbm, vx_hbm, vy_hbm, c_ref, f_ref, f_sem):
    t = pos_ref[0]
    first = jnp.minimum(jnp.maximum(2 * t - 1, 0), 2 * blocks - 4)
    begin = pl.multiple_of(first * LANES, LANES)
    copies = [
        pltpu.make_async_copy(ref.at[:, pl.ds(begin, 4 * LANES)], f_ref.at[q], f_sem.at[q])
        for q, ref in enumerate((kappa_hbm, vx_hbm, vy_hbm))
    ]
    for copy in copies:
        copy.start()
    for copy in copies:
        copy.wait()
    for q in range(3):

        def at(i):
            i = jnp.minimum(jnp.maximum(i - first, 0), 3)
            return f_ref[q, :, pl.ds(pl.multiple_of(i * LANES, LANES), LANES)]

        c_ref[q, :DEPTH] = at(2 * t)
        c_ref[q, DEPTH : 2 * DEPTH] = at(2 * t + 1)
        left = jnp.where(t > 0, at(2 * t - 1), 0.0)
        right = jnp.where(t < blocks - 1, at(2 * t + 2), 0.0)
        c_ref[q, 2 * DEPTH :] = rim(left, right, 8)


def lane_shift(tiles, lane):
    back = [pltpu.roll(v, 1, 1) for v in tiles]
    fore = [pltpu.roll(v, LANES - 1, 1) for v in tiles]
    west = [jnp.where(lane == 0, back[(c + 2) % 3], back[c]) for c in range(3)]
    east = [jnp.where(lane == LANES - 1, fore[(c + 1) % 3], fore[c]) for c in range(3)]
    return west, east


def reader(pos_ref, own_ref, chip_ref, link_ref):
    odd = lax.rem(pos_ref[1], 2) == 1

    def read(b, *at):
        if b == 1:
            return own_ref[at]
        pair = (chip_ref[at], link_ref[at])
        return jnp.where(odd, *(pair if b == 0 else pair[::-1]))

    return read


def stencil(blocks, slabs, pos_ref, own_ref, chip_ref, link_ref, out_ref):
    rows = 3 * DEPTH
    t, s = pos_ref[0], pos_ref[1]
    lane = lax.broadcasted_iota(jnp.int32, (rows, LANES), 1)
    lane8 = lax.broadcasted_iota(jnp.int32, (8, LANES), 1)
    row = lax.broadcasted_iota(jnp.int32, (rows, LANES), 0) + (s - 1) * DEPTH
    inside = (row >= 0) & (row < slabs * DEPTH)

    read = reader(pos_ref, own_ref, chip_ref, link_ref)

    def whole(q, c):
        base = c * DEPTH
        if c < 2:
            return jnp.concatenate([read(b, q, pl.ds(base, DEPTH)) for b in range(3)], axis=0)
        return jnp.concatenate(
            [unfold(read(b, q, pl.ds(base, 8)), half * (LANES // 2), lane8) for b in range(3) for half in range(2)], axis=0
        )

    kappa = [whole(0, c) for c in range(TILES)]
    west, east = lane_shift(kappa, lane)
    for c in range(TILES):
        k, vx, vy = kappa[c], whole(1, c), whole(2, c)
        north, south = pltpu.roll(k, 1, 0), pltpu.roll(k, rows - 1, 0)
        fn, fs, fw, fe = (0.5 * (k + v) for v in (north, south, west[c], east[c]))
        inverse = 1.0 / (1.0 + TAU * (fn + fs + fw + fe))
        inverse = jnp.where(inside, inverse, 0.0)
        if c == 2:
            in_right = (lane < DEPTH) & (t < blocks - 1)
            in_left = (lane >= LANES - DEPTH) & (t > 0)
            inverse = jnp.where(in_right | in_left, inverse, 0.0)
        half = 0.5 * TAU
        values = (
            (TAU * fn + half * vy) * inverse,
            (TAU * fs - half * vy) * inverse,
            (TAU * fw + half * vx) * inverse,
            (TAU * fe - half * vx) * inverse,
            inverse,
        )
        for q, v in enumerate(values):
            for r in range(rows):
                out_ref[q, r, c] = jnp.broadcast_to(v[r : r + 1], (8, LANES))


def split(v):
    high = v.astype(BF16)
    return high, (v - high.astype(F32)).astype(BF16)


def relax(n, slabs, pos_ref, own_ref, chip_ref, link_ref, coef_ref, part_ref, change_ref, first_ref, field, start, right):
    lane = lax.broadcasted_iota(jnp.int32, (n, LANES), 1)
    weights = chebyshev_weights()
    rows = 3 * DEPTH

    def wide(q, r, c):
        v = coef_ref[q, r, c]
        return jnp.concatenate([v] * (n // 8), axis=0)

    def begin(r, c, v):
        field[r, c] = v
        start[r, c] = v
        right[r, c] = v * wide(4, r, c)

    def slab(b, ref):
        for c in range(2):
            for r in range(DEPTH):
                begin(b * DEPTH + r, c, ref[pl.ds(c * DEPTH + r, n, stride=BLOCK), :])
        for r in range(4):
            folded = ref[pl.ds(2 * DEPTH + r, n, stride=BLOCK), :]
            for p in range(4):
                begin(b * DEPTH + p * 4 + r, 2, unfold(folded, p * (LANES // 4), lane))

    odd = lax.rem(pos_ref[1], 2) == 1
    slab(1, own_ref)

    @pl.when(odd)
    def _():
        slab(0, chip_ref)
        slab(2, link_ref)

    @pl.when(jnp.logical_not(odd))
    def _():
        slab(0, link_ref)
        slab(2, chip_ref)

    def sweep(k, weight):
        def one(r, north, here):
            south = [field[r + 1, c] for c in range(TILES)]
            west, east = lane_shift(here, lane)
            for c in range(TILES):
                pull = right[r, c] - here[c]
                pull += wide(0, r, c) * north[c] + wide(1, r, c) * south[c]
                pull += wide(2, r, c) * west[c] + wide(3, r, c) * east[c]
                field[r, c] = here[c] + weight * pull
            return here, south

        carried = ([field[k - 1, c] for c in range(TILES)], [field[k, c] for c in range(TILES)])
        for r in range(k, rows - k):
            carried = one(r, *carried)

    for step in range(STEPS):
        if step:
            done = step * SWEEPS

            for r in range(done + 1, rows - done - 1):
                for c in range(TILES):
                    v = (4.0 * field[r, c] - start[r, c]) / 3.0
                    right[r, c] = v * wide(4, r, c)
        for k in range(SWEEPS):
            sweep(step * SWEEPS + k + 1, weights[k])

    total = jnp.zeros((2 * n, 4 * n), F32)
    for r in range(DEPTH):
        s = jnp.concatenate([start[DEPTH + r, c] for c in range(2)], axis=1)
        e = jnp.concatenate([field[DEPTH + r, c] for c in range(2)], axis=1)
        change = e - s
        s_high, s_low = split(s)
        c_high, c_low = split(change)
        total += lax.dot_general(
            jnp.concatenate([s_high, s_low], axis=0),
            jnp.concatenate([s_high, c_high, s_low, c_low], axis=0),
            (((1,), (1,)), ((), ())),
            preferred_element_type=F32,
        )
        change_ref[:, r * 2 * LANES : (r + 1) * 2 * LANES] = jnp.concatenate([c_high, c_low], axis=0)
        first_ref[r : r + 1, :] = s[0:1]
    both = total[:n] + total[n:]
    both = both[:, : 2 * n] + both[:, 2 * n :]
    wide_both = jnp.concatenate([both] * 4, axis=1)
    lane = lax.broadcasted_iota(jnp.int32, (n, LANES), 1)
    row = lax.broadcasted_iota(jnp.int32, (n, LANES), 0)
    wide_both = jnp.where(lane // (2 * n) == row % 4, wide_both, 0.0)
    packed = [sum(wide_both[4 * q + p : 4 * q + p + 1] for p in range(4)) for q in range(n // 4)]
    packed = jnp.concatenate(packed, axis=0)
    for i in range(slabs):
        part_ref[i] = packed


def add_up(peers, in_ref, out_ref):
    total = in_ref[0]
    for i in range(1, in_ref.shape[0]):
        total += in_ref[i]
    for i in range(peers):
        out_ref[i] = total


def correct(n, in_ref, change_ref, first_ref, out_ref):
    total = in_ref[0]
    for i in range(1, n):
        total += in_ref[i]
    lane = lax.broadcasted_iota(jnp.int32, (n, LANES), 1)
    row = lax.broadcasted_iota(jnp.int32, (n, LANES), 0)
    rows = jnp.concatenate([total[k // 4 : k // 4 + 1] for k in range(n)], axis=0)
    work = jnp.where(lane // (2 * n) == row % 4, rows, 0.0)
    work += pltpu.roll(work, 2 * n, 1)
    work += pltpu.roll(work, 4 * n, 1)
    for k in range(n):
        pivot = work[k : k + 1] / work[k : k + 1, k : k + 1]
        work = jnp.where(row == k, pivot, work - work[:, k : k + 1] * pivot)
    small = functools.partial(
        lax.dot_general, precision=lax.Precision.HIGHEST, preferred_element_type=F32
    )
    plain = (((1,), (0,)), ((), ()))
    across = (((1,), (1,)), ((), ()))
    power = jnp.where(lane < n, pltpu.roll(work, LANES - n, 1), 0.0)
    power += jnp.where((lane == row) | ((lane == n) & (row == 0)), 1.0, 0.0)
    last = jnp.where((lane == n) & (row == 0), 1.0, 0.0)
    power = jnp.concatenate([power, last], axis=0)[:, : 2 * n]
    states = last[:, : 2 * n]
    step = 1
    while step < n:
        states += small(pltpu.roll(states, step, 0), power, across)
        step *= 2
        if step < n:
            power = small(power, power, plain)
    mix = states[:, :n]
    high, low = split(mix)
    left = jnp.concatenate(
        [jnp.concatenate([high, high], axis=1), jnp.concatenate([low, low], axis=1)], axis=0
    )
    for r in range(DEPTH):
        got = lax.dot_general(
            left,
            change_ref[:, r * 2 * LANES : (r + 1) * 2 * LANES],
            plain,
            preferred_element_type=F32,
        )
        got = got[:n] + got[n:] + first_ref[r : r + 1, :]
        for c in range(2):
            out_ref[pl.ds(c * DEPTH + r, n, stride=2 * DEPTH), :] = got[:, c * LANES : (c + 1) * LANES]


def spread(n, in_ref, out_ref):
    for i in range(2 * n):
        out_ref[:, i * LANES : (i + 1) * LANES] = in_ref[i]


def per_device(starts, kappa, velocity_x, velocity_y):
    n, slabs = lax.axis_size("tm"), lax.axis_size("space")
    pos = jnp.stack([lax.axis_index("tm"), lax.axis_index("space")]).astype(jnp.int32)
    shape = jax.ShapeDtypeStruct
    chip = [(i, i ^ 1) for i in range(slabs)]
    link = [(i, j) for i in range(slabs) if 0 <= (j := i + (1 if i % 2 else -1)) < slabs]

    def exchange(v, axis):
        return lax.all_to_all(v, axis, 0, 0, tiled=True)

    def neighbours(v):
        return lax.ppermute(v, "space", chip), lax.ppermute(v, "space", link)

    (blocks,) = call(functools.partial(pack, n), [shape((n * BLOCK, LANES), F32)])(starts[0])
    own = exchange(blocks.reshape(n, BLOCK // 4, 4, LANES), "tm").reshape(n * BLOCK, LANES)
    (coefs,) = call(
        functools.partial(pack_coefficients, n),
        [shape((3, COEF, LANES), F32)],
        scratch=[pltpu.VMEM((3, DEPTH, 4 * LANES), F32), pltpu.SemaphoreType.DMA((3,))],
        smem=1,
        hbm=3,
        n_in=4,
    )(pos, *(pltpu.with_memory_space_constraint(v, pltpu.HBM) for v in (kappa, velocity_x, velocity_y)))
    coef_chip, coef_link = neighbours(coefs)
    (table,) = call(
        functools.partial(stencil, n, slabs),
        [shape((5, 3 * DEPTH, TILES, 8, LANES), F32)],
        smem=1,
        n_in=4,
    )(pos, coefs, coef_chip, coef_link)
    own, table = lax.optimization_barrier((own, table))
    own_chip, own_link = neighbours(own)
    grid = pltpu.VMEM((3 * DEPTH, TILES, n, LANES), F32)
    part, change, first = call(
        functools.partial(relax, n, slabs),
        [
            shape((slabs, n // 4, LANES), F32),
            shape((2 * n, DEPTH * 2 * LANES), BF16),
            shape((DEPTH, 2 * LANES), F32),
        ],
        scratch=[grid, grid, grid],
        smem=1,
        n_in=5,
    )(pos, own, own_chip, own_link, table)
    (part,) = call(functools.partial(add_up, n), [shape((n, n // 4, LANES), F32)])(exchange(part, "space"))
    (result,) = call(
        functools.partial(correct, n),
        [shape((n * 2 * DEPTH, LANES), F32)],
        n_in=3,
    )(exchange(part, "tm"), change, first)
    result = exchange(result.reshape(n, 2, DEPTH, LANES), "tm")
    (result,) = call(functools.partial(spread, n), [shape((DEPTH, n * 2 * LANES), F32)])(
        result.reshape(2 * n, DEPTH, LANES)
    )
    return result[None]


def solution(mesh):
    in_specs = (P("tm", "space", None), P("space", None), P("space", None), P("space", None))
    out_specs = P("tm", "space", None)
    return jax.shard_map(
        per_device, mesh=mesh, in_specs=in_specs, out_specs=out_specs, check_vma=False
    )
```

```python
import functools
import math

import jax
import jax.numpy as jnp
from jax import lax
from jax.experimental import pallas as pl
from jax.experimental.pallas import tpu as pltpu
from jax.sharding import PartitionSpec as P

STEPS = 2
SWEEPS = 8
TAU = 0.4
LANES = 128
DEPTH = STEPS * SWEEPS
TILES = 3
VMEM = 48 * 2**20

F32 = jnp.float32
BF16 = jnp.bfloat16


def chebyshev_weights():
    return [
        1.0 / (1.0 - 0.8 * math.cos(math.pi * (2 * k + 1) / (2.0 * SWEEPS)))
        for k in range(SWEEPS)
    ]


def call(body, outs, scratch=(), smem=0, hbm=0, n_in=1):
    specs = [pl.BlockSpec(memory_space=pltpu.SMEM)] * smem
    specs += [pl.BlockSpec(memory_space=pltpu.HBM)] * hbm
    specs += [pl.BlockSpec(memory_space=pltpu.VMEM)] * (n_in - smem - hbm)
    return pl.pallas_call(
        body,
        out_shape=outs,
        in_specs=specs,
        out_specs=[pl.BlockSpec(memory_space=pltpu.VMEM)] * len(outs),
        scratch_shapes=list(scratch),
        compiler_params=pltpu.CompilerParams(vmem_limit_bytes=VMEM),
    )


BLOCK = 2 * DEPTH + 4
COEF = 2 * DEPTH + 8


def fold(rim, rows):
    rim = pltpu.roll(rim, DEPTH, 1)
    shift = LANES // 2
    while rim.shape[0] > rows:
        half = rim.shape[0] // 2
        rim = rim[:half] + pltpu.roll(rim[half:], shift, 1)
        shift //= 2
    return rim


def unfold(folded, shift, lane):
    rim = pltpu.roll(folded, (LANES - DEPTH - shift) % LANES, 1)
    return jnp.where((lane < DEPTH) | (lane >= LANES - DEPTH), rim, 0.0)


def rim(left, right, rows):
    lane = lax.broadcasted_iota(jnp.int32, left.shape, 1)
    return fold(jnp.where(lane < DEPTH, right, jnp.where(lane >= LANES - DEPTH, left, 0.0)), rows)


def pack(blocks, x_hbm, a_ref, x_ref, sem):
    copy = pltpu.make_async_copy(x_hbm, x_ref, sem)
    copy.start()
    copy.wait()

    def tile(j):
        inside = 0 <= j < 2 * blocks
        return x_ref[:, j * LANES : (j + 1) * LANES] if inside else jnp.zeros((DEPTH, LANES), F32)

    for k in range(blocks):
        a_ref[k * BLOCK : k * BLOCK + DEPTH] = tile(2 * k)
        a_ref[k * BLOCK + DEPTH : k * BLOCK + 2 * DEPTH] = tile(2 * k + 1)
        a_ref[k * BLOCK + 2 * DEPTH : (k + 1) * BLOCK] = rim(tile(2 * k - 1), tile(2 * k + 2), 4)


def pack_coefficients(blocks, pos_ref, kappa_hbm, vx_hbm, vy_hbm, c_ref, f_ref, f_sem):
    t = pos_ref[0]
    first = jnp.minimum(jnp.maximum(2 * t - 1, 0), 2 * blocks - 4)
    begin = pl.multiple_of(first * LANES, LANES)
    copies = [
        pltpu.make_async_copy(ref.at[:, pl.ds(begin, 4 * LANES)], f_ref.at[q], f_sem.at[q])
        for q, ref in enumerate((kappa_hbm, vx_hbm, vy_hbm))
    ]
    for copy in copies:
        copy.start()
    for copy in copies:
        copy.wait()
    for q in range(3):

        def at(i):
            i = jnp.minimum(jnp.maximum(i - first, 0), 3)
            return f_ref[q, :, pl.ds(pl.multiple_of(i * LANES, LANES), LANES)]

        c_ref[q, :DEPTH] = at(2 * t)
        c_ref[q, DEPTH : 2 * DEPTH] = at(2 * t + 1)
        left = jnp.where(t > 0, at(2 * t - 1), 0.0)
        right = jnp.where(t < blocks - 1, at(2 * t + 2), 0.0)
        c_ref[q, 2 * DEPTH :] = rim(left, right, 8)


def lane_shift(tiles, lane):
    back = [pltpu.roll(v, 1, 1) for v in tiles]
    fore = [pltpu.roll(v, LANES - 1, 1) for v in tiles]
    west = [jnp.where(lane == 0, back[(c + 2) % 3], back[c]) for c in range(3)]
    east = [jnp.where(lane == LANES - 1, fore[(c + 1) % 3], fore[c]) for c in range(3)]
    return west, east


def reader(pos_ref, own_ref, chip_ref, link_ref):
    odd = lax.rem(pos_ref[1], 2) == 1

    def read(b, *at):
        if b == 1:
            return own_ref[at]
        pair = (chip_ref[at], link_ref[at])
        return jnp.where(odd, *(pair if b == 0 else pair[::-1]))

    return read


def stencil(blocks, slabs, pos_ref, own_ref, chip_ref, link_ref, out_ref):
    rows = 3 * DEPTH
    t, s = pos_ref[0], pos_ref[1]
    lane = lax.broadcasted_iota(jnp.int32, (rows, LANES), 1)
    lane8 = lax.broadcasted_iota(jnp.int32, (8, LANES), 1)
    row = lax.broadcasted_iota(jnp.int32, (rows, LANES), 0) + (s - 1) * DEPTH
    inside = (row >= 0) & (row < slabs * DEPTH)

    read = reader(pos_ref, own_ref, chip_ref, link_ref)

    def whole(q, c):
        base = c * DEPTH
        if c < 2:
            return jnp.concatenate([read(b, q, pl.ds(base, DEPTH)) for b in range(3)], axis=0)
        return jnp.concatenate(
            [unfold(read(b, q, pl.ds(base, 8)), half * (LANES // 2), lane8) for b in range(3) for half in range(2)], axis=0
        )

    kappa = [whole(0, c) for c in range(TILES)]
    west, east = lane_shift(kappa, lane)
    for c in range(TILES):
        k, vx, vy = kappa[c], whole(1, c), whole(2, c)
        north, south = pltpu.roll(k, 1, 0), pltpu.roll(k, rows - 1, 0)
        fn, fs, fw, fe = (0.5 * (k + v) for v in (north, south, west[c], east[c]))
        inverse = 1.0 / (1.0 + TAU * (fn + fs + fw + fe))
        inverse = jnp.where(inside, inverse, 0.0)
        if c == 2:
            in_right = (lane < DEPTH) & (t < blocks - 1)
            in_left = (lane >= LANES - DEPTH) & (t > 0)
            inverse = jnp.where(in_right | in_left, inverse, 0.0)
        half = 0.5 * TAU
        values = (
            (TAU * fn + half * vy) * inverse,
            (TAU * fs - half * vy) * inverse,
            (TAU * fw + half * vx) * inverse,
            (TAU * fe - half * vx) * inverse,
            inverse,
        )
        for q, v in enumerate(values):
            for r in range(rows):
                out_ref[q, r, c] = jnp.broadcast_to(v[r : r + 1], (8, LANES))


def split(v):
    high = v.astype(BF16)
    return high, (v - high.astype(F32)).astype(BF16)


def relax(n, slabs, pos_ref, own_ref, chip_ref, link_ref, coef_ref, part_ref, change_ref, first_ref, field, start, right):
    lane = lax.broadcasted_iota(jnp.int32, (n, LANES), 1)
    weights = chebyshev_weights()
    rows = 3 * DEPTH

    def wide(q, r, c):
        v = coef_ref[q, r, c]
        return jnp.concatenate([v] * (n // 8), axis=0)

    def begin(r, c, v):
        field[r, c] = v
        start[r, c] = v
        right[r, c] = v * wide(4, r, c)

    def slab(b, ref):
        for c in range(2):
            for r in range(DEPTH):
                begin(b * DEPTH + r, c, ref[pl.ds(c * DEPTH + r, n, stride=BLOCK), :])
        for r in range(4):
            folded = ref[pl.ds(2 * DEPTH + r, n, stride=BLOCK), :]
            for p in range(4):
                begin(b * DEPTH + p * 4 + r, 2, unfold(folded, p * (LANES // 4), lane))

    odd = lax.rem(pos_ref[1], 2) == 1
    slab(1, own_ref)

    @pl.when(odd)
    def _():
        slab(0, chip_ref)
        slab(2, link_ref)

    @pl.when(jnp.logical_not(odd))
    def _():
        slab(0, link_ref)
        slab(2, chip_ref)

    def sweep(k, weight):
        def one(r, north, here):
            south = [field[r + 1, c] for c in range(TILES)]
            west, east = lane_shift(here, lane)
            for c in range(TILES if k < DEPTH else 2):
                pull = right[r, c] - here[c]
                pull += wide(0, r, c) * north[c] + wide(1, r, c) * south[c]
                pull += wide(2, r, c) * west[c] + wide(3, r, c) * east[c]
                field[r, c] = here[c] + weight * pull
            return here, south

        carried = ([field[k - 1, c] for c in range(TILES)], [field[k, c] for c in range(TILES)])
        for r in range(k, rows - k):
            carried = one(r, *carried)

    for step in range(STEPS):
        if step:
            done = step * SWEEPS

            for r in range(done + 1, rows - done - 1):
                for c in range(TILES):
                    right[r, c] = (4.0 * field[r, c] - start[r, c]) * (wide(4, r, c) * (1.0 / 3.0))
        for k in range(SWEEPS):
            sweep(step * SWEEPS + k + 1, weights[k])

    total = jnp.zeros((2 * n, 4 * n), F32)
    for r in range(DEPTH):
        s = jnp.concatenate([start[DEPTH + r, c] for c in range(2)], axis=1)
        e = jnp.concatenate([field[DEPTH + r, c] for c in range(2)], axis=1)
        change = e - s
        s_high, s_low = split(s)
        c_high, c_low = split(change)
        total += lax.dot_general(
            jnp.concatenate([s_high, s_low], axis=0),
            jnp.concatenate([s_high, c_high, s_low, c_low], axis=0),
            (((1,), (1,)), ((), ())),
            preferred_element_type=F32,
        )
        change_ref[:, r * 2 * LANES : (r + 1) * 2 * LANES] = jnp.concatenate([c_high, c_low], axis=0)
        first_ref[r : r + 1, :] = s[0:1]
    both = total[:n] + total[n:]
    both = both[:, : 2 * n] + both[:, 2 * n :]
    wide_both = jnp.concatenate([both] * 4, axis=1)
    lane = lax.broadcasted_iota(jnp.int32, (n, LANES), 1)
    row = lax.broadcasted_iota(jnp.int32, (n, LANES), 0)
    wide_both = jnp.where(lane // (2 * n) == row % 4, wide_both, 0.0)
    packed = [sum(wide_both[4 * q + p : 4 * q + p + 1] for p in range(4)) for q in range(n // 4)]
    packed = jnp.concatenate(packed, axis=0)
    for i in range(slabs):
        part_ref[i] = packed


def add_up(peers, in_ref, out_ref):
    total = in_ref[0]
    for i in range(1, in_ref.shape[0]):
        total += in_ref[i]
    for i in range(peers):
        out_ref[i] = total


def correct(n, in_ref, change_ref, first_ref, out_ref):
    total = in_ref[0]
    for i in range(1, n):
        total += in_ref[i]
    lane = lax.broadcasted_iota(jnp.int32, (n, LANES), 1)
    row = lax.broadcasted_iota(jnp.int32, (n, LANES), 0)
    rows = jnp.concatenate([total[k // 4 : k // 4 + 1] for k in range(n)], axis=0)
    work = jnp.where(lane // (2 * n) == row % 4, rows, 0.0)
    work += pltpu.roll(work, 2 * n, 1)
    work += pltpu.roll(work, 4 * n, 1)
    for k in range(n):
        pivot = work[k : k + 1] / work[k : k + 1, k : k + 1]
        work = jnp.where(row == k, pivot, work - work[:, k : k + 1] * pivot)
    small = functools.partial(
        lax.dot_general, precision=lax.Precision.HIGHEST, preferred_element_type=F32
    )
    plain = (((1,), (0,)), ((), ()))
    across = (((1,), (1,)), ((), ()))
    power = jnp.where(lane < n, pltpu.roll(work, LANES - n, 1), 0.0)
    power += jnp.where((lane == row) | ((lane == n) & (row == 0)), 1.0, 0.0)
    last = jnp.where((lane == n) & (row == 0), 1.0, 0.0)
    power = jnp.concatenate([power, last], axis=0)[:, : 2 * n]
    states = last[:, : 2 * n]
    step = 1
    while step < n:
        states += small(pltpu.roll(states, step, 0), power, across)
        step *= 2
        if step < n:
            power = small(power, power, plain)
    mix = states[:, :n]
    high, low = split(mix)
    left = jnp.concatenate(
        [jnp.concatenate([high, high], axis=1), jnp.concatenate([low, low], axis=1)], axis=0
    )
    for r in range(DEPTH):
        got = lax.dot_general(
            left,
            change_ref[:, r * 2 * LANES : (r + 1) * 2 * LANES],
            plain,
            preferred_element_type=F32,
        )
        got = got[:n] + got[n:] + first_ref[r : r + 1, :]
        for c in range(2):
            out_ref[pl.ds(c * DEPTH + r, n, stride=2 * DEPTH), :] = got[:, c * LANES : (c + 1) * LANES]


def spread(n, in_ref, out_ref):
    for i in range(2 * n):
        out_ref[:, i * LANES : (i + 1) * LANES] = in_ref[i]


def per_device(starts, kappa, velocity_x, velocity_y):
    n, slabs = lax.axis_size("tm"), lax.axis_size("space")
    pos = jnp.stack([lax.axis_index("tm"), lax.axis_index("space")]).astype(jnp.int32)
    shape = jax.ShapeDtypeStruct
    chip = [(i, i ^ 1) for i in range(slabs)]
    link = [(i, j) for i in range(slabs) if 0 <= (j := i + (1 if i % 2 else -1)) < slabs]

    def exchange(v, axis):
        return lax.all_to_all(v, axis, 0, 0, tiled=True)

    def neighbours(v):
        return lax.ppermute(v, "space", chip), lax.ppermute(v, "space", link)

    (blocks,) = call(
        functools.partial(pack, n),
        [shape((n * BLOCK, LANES), F32)],
        scratch=[pltpu.VMEM(starts.shape[1:], F32), pltpu.SemaphoreType.DMA],
        hbm=1,
    )(pltpu.with_memory_space_constraint(starts[0], pltpu.HBM))
    own = exchange(blocks.reshape(n, BLOCK // 4, 4, LANES), "tm").reshape(n * BLOCK, LANES)
    (coefs,) = call(
        functools.partial(pack_coefficients, n),
        [shape((3, COEF, LANES), F32)],
        scratch=[pltpu.VMEM((3, DEPTH, 4 * LANES), F32), pltpu.SemaphoreType.DMA((3,))],
        smem=1,
        hbm=3,
        n_in=4,
    )(pos, *(pltpu.with_memory_space_constraint(v, pltpu.HBM) for v in (kappa, velocity_x, velocity_y)))
    coef_chip, coef_link = neighbours(coefs)
    (table,) = call(
        functools.partial(stencil, n, slabs),
        [shape((5, 3 * DEPTH, TILES, 8, LANES), F32)],
        smem=1,
        n_in=4,
    )(pos, coefs, coef_chip, coef_link)
    own, table = lax.optimization_barrier((own, table))
    own_chip, own_link = neighbours(own)
    grid = pltpu.VMEM((3 * DEPTH, TILES, n, LANES), F32)
    part, change, first = call(
        functools.partial(relax, n, slabs),
        [
            shape((slabs, n // 4, LANES), F32),
            shape((2 * n, DEPTH * 2 * LANES), BF16),
            shape((DEPTH, 2 * LANES), F32),
        ],
        scratch=[grid, grid, grid],
        smem=1,
        n_in=5,
    )(pos, own, own_chip, own_link, table)
    (part,) = call(functools.partial(add_up, n), [shape((n, n // 4, LANES), F32)])(exchange(part, "space"))
    (result,) = call(
        functools.partial(correct, n),
        [shape((n * 2 * DEPTH, LANES), F32)],
        n_in=3,
    )(exchange(part, "tm"), change, first)
    result = exchange(result.reshape(n, 2, DEPTH, LANES), "tm")
    (result,) = call(functools.partial(spread, n), [shape((DEPTH, n * 2 * LANES), F32)])(
        result.reshape(2 * n, DEPTH, LANES)
    )
    return result[None]


def solution(mesh):
    in_specs = (P("tm", "space", None), P("space", None), P("space", None), P("space", None))
    out_specs = P("tm", "space", None)
    return jax.shard_map(
        per_device, mesh=mesh, in_specs=in_specs, out_specs=out_specs, check_vma=False
    )
```
